512 devices in a mesh: grp: 16 (over x_hi, y, core), dev: 32 (over x_lo, z).
Axes of the slice: x: 4 (x_hi: 2, x_lo: 2; x = x_hi * 2 + x_lo), y: 4, z: 16, core: 2. Of those that a mesh axis runs over, the one named last changes fastest.
Arguments:
- states: bfloat16 [2, 512, 128, 4096], P(None, ('grp', 'dev')), may hold values from -64 to 64
- lengths: int32 [2, 512], replicated, may hold values from 32 to 128
Outputs:
- utility: float32 [2, 512], P(None, ('grp', 'dev'))
- best_match: float32 [2, 512, 128], P(None, ('grp', 'dev'))
The draws below stay inside these ranges and needn't reach their ends.
All inputs are finite; a program needn't handle non-finite values.
Results may differ from the reference program's by a relative error of at most 0.00059.
Values may be sent and summed in bfloat16 or wider, within the bound.
No kernel may reach another device: no remote copies, remote signals or barrier semaphores. Data moves between devices by JAX's collectives and lax.ppermute only.
A program may use at most 64 MiB of HBM per device.

```python
import jax
import jax.numpy as jnp
import numpy as np
from jax import lax

D = 4096
L = 128
PROMPTS = 2
ROUNDS = 2
CANDS = 512
N_GRP = 16
N_DEV = 32


def draw_states(key, part):
    key = jax.random.fold_in(key, 11)
    keys = jax.random.split(key, 8)
    vocabulary_ids = 128
    token_ids = jax.random.randint(keys[7], (PROMPTS, CANDS, L), 0, vocabulary_ids, jnp.int32)
    prompt_index = jnp.arange(PROMPTS, dtype=jnp.int32)[:, None, None]
    base = jax.random.normal(keys[0], (PROMPTS, 1, 1, D), jnp.float32)
    candidate = 0.6 * jax.random.normal(keys[1], (PROMPTS, CANDS, 1, D), jnp.float32)
    noise = jax.random.normal(keys[2], (PROMPTS, CANDS, L, D), jnp.float32)
    mixing = jax.random.uniform(keys[3], (PROMPTS, CANDS, L, 1), jnp.float32, 0.3, 1.8)
    row_scale = jnp.exp(jax.random.uniform(keys[4], (PROMPTS, CANDS, L, 1), jnp.float32, -1.2, 1.2))
    feature_scale = jnp.exp(jax.random.uniform(keys[5], (1, 1, 1, D), jnp.float32, -1.2, 1.2))
    vocabulary = jax.random.normal(keys[6], (PROMPTS, vocabulary_ids, D), jnp.float32)
    lexical = 2.0 * vocabulary[prompt_index, token_ids]
    values = row_scale * feature_scale * (mixing * base + candidate + noise + lexical)
    return jnp.clip(values, -64.0, 64.0).astype(jnp.bfloat16)


def draw_lengths(key, part):
    key = jax.random.fold_in(key, 23)
    keys = jax.random.split(key, 3)
    total = PROMPTS * CANDS
    values = jax.random.randint(keys[0], (total,), L // 4, L + 1, jnp.int32)
    spot_high = jax.random.randint(keys[1], (), 0, total, jnp.int32)
    spot_low = (spot_high + 1 + jax.random.randint(keys[2], (), 0, total - 1, jnp.int32)) % total
    values = values.at[spot_high].set(L)
    values = values.at[spot_low].set(L // 4)
    return values.reshape(PROMPTS, CANDS)


def setup_inputs(seed: int = 0) -> dict:
    seeds = jax.random.split(jax.random.key(seed), 3)
    states = draw_states(jax.random.fold_in(seeds[2], 71), 0)
    lengths = draw_lengths(jax.random.fold_in(seeds[2], 71), 0)
    return {"states": states, "lengths": lengths}


epsilon = 1e-06
sentinel = -4.0

def normalize(states):
    values = states.astype(jnp.float32)
    inverse_norm = lax.rsqrt(lax.optimization_barrier(jnp.sum(values * values, axis=-1, keepdims=True)) + epsilon)
    return (values * inverse_norm).astype(jnp.bfloat16)

def pair_scores(pair_items):
    first_block, second_block, first_len, second_len = pair_items
    similarity = jnp.dot(first_block, second_block.T, preferred_element_type=jnp.float32)
    positions = jnp.arange(L, dtype=jnp.int32)
    first_valid = positions < first_len
    second_valid = positions < second_len
    row_best = lax.optimization_barrier(jnp.max(jnp.where(second_valid[None, :], similarity, sentinel), axis=1))
    column_best = lax.optimization_barrier(jnp.max(jnp.where(first_valid[:, None], similarity, sentinel), axis=0))
    precision = jnp.sum(jnp.where(first_valid, row_best, 0.0)) / first_len.astype(jnp.float32)
    recall = jnp.sum(jnp.where(second_valid, column_best, 0.0)) / second_len.astype(jnp.float32)
    pair_score = 0.5 * (precision + recall)
    return (row_best, column_best, pair_score)

def reference(states, lengths):
    unit_states = normalize(states)
    cand_total = N_GRP * N_DEV
    utility = jnp.zeros((PROMPTS, cand_total), jnp.float32)
    best_match = jnp.full((PROMPTS, cand_total, L), sentinel, jnp.float32)
    group_ids = np.arange(N_GRP)
    member_ids = np.arange(N_DEV)
    for round_index in range(ROUNDS):
        stride = 2 ** round_index
        lower_groups = group_ids[group_ids // stride % 2 == 0]
        for prompt in range(PROMPTS):
            for offset in range(-2 - prompt, 4 - prompt):
                lower_cands = (lower_groups[:, None] * N_DEV + member_ids[None, :]).reshape(-1).astype(np.int32)
                upper_cands = ((lower_groups[:, None] + stride) * N_DEV + (member_ids[None, :] + offset) % N_DEV).reshape(-1).astype(np.int32)
                first_states = unit_states[prompt, lower_cands]
                second_states = unit_states[prompt, upper_cands]
                first_lens = lengths[prompt, lower_cands]
                second_lens = lengths[prompt, upper_cands]
                row_best, column_best, pair_score = lax.map(pair_scores, (first_states, second_states, first_lens, second_lens))
                utility = utility.at[prompt, lower_cands].add(pair_score)
                utility = utility.at[prompt, upper_cands].add(pair_score)
                best_match = best_match.at[prompt, lower_cands].max(row_best)
                best_match = best_match.at[prompt, upper_cands].max(column_best)
    token_valid = jnp.arange(L, dtype=jnp.int32)[None, None, :] < lengths[:, :, None]
    best_match = jnp.where(token_valid, best_match, 0.0)
    return (utility, best_match)
```

```python
import functools

import jax
import jax.numpy as jnp
from jax import lax
from jax.experimental import pallas as pl
from jax.experimental.pallas import tpu as pltpu
from jax.sharding import PartitionSpec as P


epsilon = 1e-06
sentinel = -4.0


def is_mid(g):
    return (g % 2) ^ (g // 2 % 2) == 1


def side(g):
    return 1 - 2 * (g // 2 % 2)


def move(value, target):
    groups, members = lax.axis_size("grp"), lax.axis_size("dev")
    pairs = []
    for g in range(groups):
        for i in range(members):
            to = target(g, i)
            if to is not None:
                pairs.append((g * members + i, to[0] * members + to[1] % members))
    return lax.ppermute(value, ("grp", "dev"), pairs)


def along(by, mids_only):
    def target(g, i):
        return (g, i + side(g) * by) if is_mid(g) or not mids_only else None

    return target


def to_mid(mask):
    return lambda g, i: None if is_mid(g) else (g ^ mask, i)


def to_outer(mask):
    return lambda g, i: (g ^ mask, i) if is_mid(g) else None


def last_move(g, i):
    return (g, i + side(g) * (2 if is_mid(g) else 1))


def normalize_kernel(flag_ref, states_ref, both_ref, first_ref, second_ref, mixed_ref):
    units = []
    for prompt in range(2):
        values = states_ref[prompt].astype(jnp.float32)
        total = jnp.sum(values * values, axis=-1, keepdims=True)
        units.append((values * lax.rsqrt(total + epsilon)).astype(jnp.bfloat16))
        both_ref[prompt] = units[prompt]
    first_ref[...] = units[0]
    second_ref[...] = units[1]

    @pl.when(flag_ref[0] == 1)
    def _():
        mixed_ref[...] = units[0]

    @pl.when(flag_ref[0] == 0)
    def _():
        mixed_ref[...] = units[1]


def normalize(flag, states):
    _, tokens, width = states.shape
    step = 32
    block = pl.BlockSpec((2, step, width), lambda i: (0, i, 0))
    flat = pl.BlockSpec((step, width), lambda i: (i, 0))
    one = jax.ShapeDtypeStruct((tokens, width), jnp.bfloat16)
    return pl.pallas_call(
        normalize_kernel,
        grid=(tokens // step,),
        in_specs=[pl.BlockSpec(memory_space=pltpu.SMEM), block],
        out_specs=[block, flat, flat, flat],
        out_shape=[jax.ShapeDtypeStruct(states.shape, jnp.bfloat16), one, one, one],
        compiler_params=pltpu.CompilerParams(vmem_limit_bytes=32 * 1024 * 1024),
        name="normalize",
    )(flag, states)


def pair_stats(similarity, x_len, m_len):
    down = lax.broadcasted_iota(jnp.int32, similarity.shape, 0)
    lane = lax.broadcasted_iota(jnp.int32, (1, similarity.shape[1]), 1)
    m_best = jnp.max(jnp.where(down < x_len, similarity, sentinel), axis=0, keepdims=True)
    x_best = jnp.max(jnp.where(down < m_len, similarity.T, sentinel), axis=0, keepdims=True)
    x_sum = jnp.sum(jnp.where(lane < x_len, x_best, 0.0), axis=1, keepdims=True)
    m_sum = jnp.sum(jnp.where(lane < m_len, m_best, 0.0), axis=1, keepdims=True)
    x_count = jnp.full((1, 1), x_len, jnp.int32).astype(jnp.float32)
    m_count = jnp.full((1, 1), m_len, jnp.int32).astype(jnp.float32)
    score = 0.5 * (x_sum / x_count + m_sum / m_count)
    return x_best, m_best, jnp.broadcast_to(score, x_best.shape)


def score_kernel(plan, x_count, m_count, assemble, lens_ref, *refs):
    x_refs = refs[:x_count]
    m_refs = refs[x_count : x_count + m_count]
    rest = refs[x_count + m_count : -m_count]
    sums = refs[-m_count:]
    step = pl.program_id(0)
    tokens = m_refs[0].shape[-2]

    def rows(ref):
        return ref[0] if len(ref.shape) == 3 else ref[...]

    for m in range(m_count):
        stack = jnp.concatenate([rows(x_refs[x]) for x in plan[m]], axis=0)
        part = lax.dot_general(
            stack, rows(m_refs[m]), (((1,), (1,)), ((), ())), preferred_element_type=jnp.float32
        )

        @pl.when(step == 0)
        def _():
            sums[m][...] = part

        @pl.when(step > 0)
        def _():
            sums[m][...] += part

    @pl.when(step == pl.num_programs(0) - 1)
    def _():
        x_best, x_sum = [None] * x_count, [None] * x_count
        m_best, m_sum = [None] * m_count, [None] * m_count

        def join(bests, totals, at, best, score):
            bests[at] = best if bests[at] is None else jnp.maximum(bests[at], best)
            totals[at] = score if totals[at] is None else totals[at] + score

        for m in range(m_count):
            for place, x in enumerate(plan[m]):
                similarity = sums[m][place * tokens : (place + 1) * tokens, :]
                x_row, m_row, score = pair_stats(similarity, lens_ref[x], lens_ref[x_count + m])
                join(x_best, x_sum, x, x_row, score)
                join(m_best, m_sum, m, m_row, score)
        assemble(x_best, x_sum, m_best, m_sum, *rest)


def score(name, plan, lens, x_blocks, m_blocks, assemble, tables, out_rows):
    chunks = 4
    blocks = list(x_blocks) + list(m_blocks)
    arrays, specs = [], []
    for block in blocks:
        if isinstance(block, tuple):
            array, prompt = block
            _, tokens, width = array.shape
            specs.append(
                pl.BlockSpec((1, tokens, width // chunks), functools.partial(lambda p, i: (p, 0, i), prompt))
            )
        else:
            array = block
            tokens, width = array.shape
            specs.append(pl.BlockSpec((tokens, width // chunks), lambda i: (0, i)))
        arrays.append(array)
    pairs = sum(len(p) for p in plan)
    whole = [pl.BlockSpec(table.shape, lambda i: (0, 0)) for table in tables]
    return pl.pallas_call(
        functools.partial(score_kernel, plan, len(x_blocks), len(m_blocks), assemble),
        grid=(chunks,),
        in_specs=[pl.BlockSpec(memory_space=pltpu.SMEM)] + specs + whole,
        out_specs=[pl.BlockSpec((r, tokens), lambda i: (0, 0)) for r in out_rows],
        out_shape=[jax.ShapeDtypeStruct((r, tokens), jnp.float32) for r in out_rows],
        scratch_shapes=[pltpu.VMEM((len(p) * tokens, tokens), jnp.float32) for p in plan],
        cost_estimate=pl.CostEstimate(
            flops=2 * pairs * tokens * tokens * width,
            bytes_accessed=2 * len(blocks) * tokens * width,
            transcendentals=0,
        ),
        compiler_params=pltpu.CompilerParams(vmem_limit_bytes=32 * 1024 * 1024),
        name=name,
    )(lens, *arrays, *tables)


def write_near(x_best, x_sum, m_best, m_sum, out_ref):
    rows = [x_best[0], x_sum[0], x_best[1], x_sum[1]]
    for m in range(3):
        rows += [m_best[m], m_sum[m]]
    out_ref[...] = jnp.concatenate(rows + [jnp.zeros_like(rows[0])] * 6, axis=0)


def write_far_first(x_best, x_sum, m_best, m_sum, near0, near1, forth_ref, back_ref, far_ref):
    zero = jnp.zeros_like(x_best[0])
    forth = [near0[8:9], near1[8:9], near0[9:10], near1[9:10], x_best[3], x_sum[3], zero, zero]
    back = [near0[6:7], near1[6:7], near0[7:8], near1[7:8], x_best[2], x_sum[2], zero, zero]
    far = [x_best[0], x_sum[0], x_best[1], x_sum[1], m_best[0], m_sum[0], m_best[1], m_sum[1]]
    forth_ref[...] = jnp.concatenate(forth, axis=0)
    back_ref[...] = jnp.concatenate(back, axis=0)
    far_ref[...] = jnp.concatenate(far, axis=0)


def write_far_second(
    x_best, x_sum, m_best, m_sum, near0, near1, far, forth, back, core_ref, cross_ref, behind_ref, ahead_ref
):
    zero = jnp.zeros_like(x_best[0])
    for x, carried, out_ref in ((0, back, core_ref), (1, forth, cross_ref)):
        best, total = slice(2 * x, 2 * x + 1), slice(2 * x + 1, 2 * x + 2)
        out_ref[...] = jnp.concatenate(
            [
                jnp.maximum(jnp.maximum(near0[best], far[best]), carried[4:5]),
                jnp.maximum(near1[best], x_best[x]),
                near0[total] + far[total] + carried[5:6],
                near1[total] + x_sum[x],
                x_best[2 + x],
                x_sum[2 + x],
                zero,
                zero,
            ],
            axis=0,
        )
    for m, out_ref in ((0, behind_ref), (1, ahead_ref)):
        best, total = slice(4 + 2 * m, 5 + 2 * m), slice(5 + 2 * m, 6 + 2 * m)
        out_ref[...] = jnp.concatenate(
            [far[best], m_best[m], far[total], m_sum[m], zero, zero, zero, zero], axis=0
        )


def body(states, lengths):
    tokens = states.shape[2]
    candidates = lengths.shape[1]
    members = lax.axis_size("dev")
    group = lax.axis_index("grp")
    member = lax.axis_index("dev")
    high = group // 2 % 2
    mid = (group % 2) ^ high
    direction = 1 - 2 * high

    both, first, second, mixed = normalize(jnp.reshape(mid, (1,)).astype(jnp.int32), states[:, 0])

    behind1_first = move(first, along(1, False))
    ahead1_mixed = move(mixed, along(-1, False))
    cross = move(both, to_mid(2))
    behind1_second = move(second, along(1, True))
    ahead1_second = move(second, along(-1, True))
    core = move(both, to_mid(1))
    behind2_first = move(behind1_first, along(1, True))
    cross_next_first = move(behind1_first, to_mid(2))
    core_next_first = move(behind1_first, to_mid(1))
    ahead2_first = move(ahead1_mixed, along(-1, True))
    cross_next_second = move(ahead1_mixed, to_mid(2))
    core_next_second = move(ahead1_mixed, to_mid(1))
    behind2_second = move(behind1_second, along(1, True))
    ahead2_second = move(ahead1_second, along(-1, True))

    def wanted(prompt, which, place):
        return prompt * candidates + which * members + (member + direction * place) % members

    core_group, cross_group = group ^ 1, group ^ 2
    slots = []
    for prompt in range(2):
        slots += [wanted(prompt, core_group, 0), wanted(prompt, cross_group, 0)]
        slots += [wanted(prompt, group, 0), wanted(prompt, group, -1), wanted(prompt, group, 1)]
        turn = 1 if prompt == 0 else -1
        slots += [wanted(prompt, core_group, 0), wanted(prompt, cross_group, 0)]
        slots += [wanted(prompt, core_group, -turn), wanted(prompt, cross_group, turn)]
        slots += [wanted(prompt, group, -2), wanted(prompt, group, 2)]
    flat = lengths.reshape(1, -1)
    chosen = jnp.stack(slots)[:, None] == lax.broadcasted_iota(jnp.int32, (1, flat.shape[1]), 1)
    lens = jnp.sum(jnp.where(chosen, flat, 0), axis=1)

    (near0,) = score(
        "near_first", [[0, 1]] * 3, lens[0:5], [(core, 0), (cross, 0)],
        [first, behind1_first, ahead1_mixed], write_near, [], [16],
    )
    (near1,) = score(
        "near_second", [[0, 1]] * 3, lens[11:16], [(core, 1), (cross, 1)],
        [second, behind1_second, ahead1_second], write_near, [], [16],
    )
    forth, back, far = score(
        "far_first", [[0, 1, 3], [0, 1, 2]], lens[5:11],
        [(core, 0), (cross, 0), core_next_first, cross_next_first],
        [behind2_first, ahead2_first], write_far_first, [near0, near1], [8, 8, 8],
    )
    forth = move(forth, along(1, True))
    back = move(back, along(-1, True))
    to_core, to_cross, behind, ahead = score(
        "far_second", [[0, 1, 2], [0, 1, 3]], lens[16:22],
        [(core, 1), (cross, 1), core_next_second, cross_next_second],
        [behind2_second, ahead2_second], write_far_second, [near0, near1, far, forth, back], [8, 8, 8, 8],
    )
    to_core = move(to_core, to_outer(1))
    to_cross = move(to_cross, to_outer(2))
    behind = move(behind, along(-2, True))
    nothing = jnp.full((1, tokens), sentinel, jnp.float32)
    none = jnp.zeros((1, tokens), jnp.float32)
    handed = jnp.concatenate(
        [nothing, jnp.maximum(to_core[4:5], to_cross[4:5]), none, to_core[5:6] + to_cross[5:6], none, none, none, none]
    )
    is_mid_here = mid == 1
    ahead = move(jnp.where(is_mid_here, ahead, handed), last_move)

    own_best = jnp.concatenate([near0[4:5], near1[4:5]])
    own_sum = jnp.concatenate([near0[5:6], near1[5:6]])
    mid_best = jnp.maximum(jnp.maximum(own_best, forth[0:2]), jnp.maximum(back[0:2], behind[0:2]))
    mid_sum = own_sum + forth[2:4] + back[2:4] + behind[2:4]
    best = jnp.where(is_mid_here, mid_best, jnp.maximum(to_core[0:2], to_cross[0:2]))
    total = jnp.where(is_mid_here, mid_sum, to_core[2:4] + to_cross[2:4])
    best = jnp.maximum(best, ahead[0:2])
    total = total + ahead[2:4]

    own = group * members + member
    columns = lax.broadcasted_iota(jnp.int32, lengths.shape, 1)
    own_lengths = jnp.sum(jnp.where(columns == own, lengths, 0), axis=1)
    token_valid = lax.broadcasted_iota(jnp.int32, (1, tokens), 1) < own_lengths[:, None]
    best = jnp.where(token_valid, best, 0.0)
    return (total[:, :1], best[:, None, :])


def solution(mesh):
    in_specs = (P(None, ("grp", "dev"), None, None), P())
    out_specs = (P(None, ("grp", "dev")), P(None, ("grp", "dev"), None))
    return jax.shard_map(body, mesh=mesh, in_specs=in_specs, out_specs=out_specs, check_vma=False)
```

```python
import functools

import jax
import jax.numpy as jnp
from jax import lax
from jax.experimental import pallas as pl
from jax.experimental.pallas import tpu as pltpu
from jax.sharding import PartitionSpec as P


epsilon = 1e-06
sentinel = -4.0
VMEM_LIMIT = 24 * 1024 * 1024


def is_mid(g):
    return (g % 2) ^ (g // 2 % 2) == 1


def sign(g):
    return 2 * (g % 2) - 1


def send_home(value, way):
    groups, members = lax.axis_size("grp"), lax.axis_size("dev")
    pairs = []
    for g in range(groups):
        by = way * (1 - 2 * (g // 2 % 2)) * (2 if is_mid(g) else 1)
        for i in range(members):
            pairs.append((g * members + i, g * members + (i + by) % members))
    return lax.ppermute(value, ("grp", "dev"), pairs)


def move(value, by, mask=0):
    groups, members = lax.axis_size("grp"), lax.axis_size("dev")
    pairs = []
    for g in range(groups):
        for i in range(members):
            pairs.append((g * members + i, (g ^ mask) * members + (i + sign(g) * by) % members))
    return lax.ppermute(value, ("grp", "dev"), pairs)


def gather(value, size):
    groups = lax.axis_size("grp")
    return lax.all_gather(
        value, "grp", axis_index_groups=[list(range(g, g + size)) for g in range(0, groups, size)]
    )


def after(value, *done):
    return lax.optimization_barrier((value, *done))


def pick_kernel(flags_ref, states_ref, out_ref, sem):
    copy = pltpu.make_async_copy(states_ref.at[flags_ref[0]], out_ref, sem)
    copy.start()
    copy.wait()


def pick(flags, states):
    anywhere = pl.BlockSpec(memory_space=pl.ANY)
    return pl.pallas_call(
        pick_kernel,
        in_specs=[pl.BlockSpec(memory_space=pltpu.SMEM), anywhere],
        out_specs=pl.BlockSpec(memory_space=pltpu.VMEM),
        out_shape=jax.ShapeDtypeStruct(states.shape[1:], states.dtype),
        scratch_shapes=[pltpu.SemaphoreType.DMA],
        name="pick",
    )(flags, states)


def normalize_kernel(flags_ref, states_ref, given_ref, m_ref, c_ref, loaded, unit, load_sems, sems):
    steps = load_sems.shape[0]
    size = loaded.shape[1] // steps
    mid = flags_ref[0]

    def loads(step):
        rows = pl.ds(step * size, size)
        return (
            pltpu.make_async_copy(states_ref.at[1 - mid, rows], loaded.at[0, rows], load_sems.at[step, 0]),
            pltpu.make_async_copy(given_ref.at[rows], loaded.at[1, rows], load_sems.at[step, 1]),
        )

    def stores(step):
        rows = pl.ds(step * size, size)
        return (
            pltpu.make_async_copy(unit.at[1 - mid, rows], m_ref.at[rows], sems.at[step, 0]),
            pltpu.make_async_copy(unit.at[mid, rows], c_ref.at[rows], sems.at[step, 1]),
        )

    for step in range(steps):
        for copy in loads(step):
            copy.start()
    for step in range(steps):
        for copy in loads(step):
            copy.wait()
        rows = pl.ds(step * size, size)
        for at in range(2):
            values = loaded[at, rows].astype(jnp.float32)
            total = jnp.sum(values * values, axis=-1, keepdims=True)
            unit[at, rows] = (values * lax.rsqrt(total + epsilon)).astype(jnp.bfloat16)
        for copy in stores(step):
            copy.start()
    for step in range(steps):
        for copy in stores(step):
            copy.wait()


def normalize(flags, states, given):
    _, tokens, width = states.shape
    steps = 4
    one = jax.ShapeDtypeStruct((tokens, width), jnp.bfloat16)
    anywhere = pl.BlockSpec(memory_space=pl.ANY)
    return pl.pallas_call(
        normalize_kernel,
        in_specs=[pl.BlockSpec(memory_space=pltpu.SMEM), anywhere, anywhere],
        out_specs=[anywhere] * 2,
        out_shape=[one, one],
        scratch_shapes=[
            pltpu.VMEM(states.shape, jnp.bfloat16),
            pltpu.VMEM(states.shape, jnp.bfloat16),
            pltpu.SemaphoreType.DMA((steps, 2)),
            pltpu.SemaphoreType.DMA((steps, 2)),
        ],
        compiler_params=pltpu.CompilerParams(vmem_limit_bytes=VMEM_LIMIT),
        name="normalize",
    )(flags, states, given)


def pair_stats(similarity, x_len, m_len):
    down = lax.broadcasted_iota(jnp.int32, similarity.shape, 0)
    lane = lax.broadcasted_iota(jnp.int32, (1, similarity.shape[1]), 1)
    x_best = jnp.max(jnp.where(down < m_len, similarity, sentinel), axis=0, keepdims=True)
    m_best = jnp.max(jnp.where(down < x_len, similarity.T, sentinel), axis=0, keepdims=True)
    x_sum = jnp.sum(jnp.where(lane < x_len, x_best, 0.0), axis=1, keepdims=True)
    m_sum = jnp.sum(jnp.where(lane < m_len, m_best, 0.0), axis=1, keepdims=True)
    x_count = jnp.full((1, 1), x_len, jnp.int32).astype(jnp.float32)
    m_count = jnp.full((1, 1), m_len, jnp.int32).astype(jnp.float32)
    score = 0.5 * (x_sum / x_count + m_sum / m_count)
    return x_best, m_best, jnp.broadcast_to(score, x_best.shape)


def score_kernel(plan, at, x_count, m_count, out_count, assemble, slots_ref, *refs):
    sources = refs[: x_count + m_count]
    tables = refs[x_count + m_count : -3 - out_count]
    outs = refs[-3 - out_count : -3]
    x_stack, m_stack, sems = refs[-3:]
    tokens, width = sources[0].shape
    halves = sems.shape[1]
    size = width // halves

    def load(block, half):
        stack, row = (x_stack, block) if block < x_count else (m_stack, block - x_count)
        columns = pl.ds(half * size, size)
        return pltpu.make_async_copy(
            sources[block].at[:, columns], stack.at[pl.ds(row * tokens, tokens), columns], sems.at[block, half]
        )

    for half in range(halves):
        for block in range(x_count + m_count):
            load(block, half).start()
    similarity = None
    for half in range(halves):
        for block in range(x_count + m_count):
            load(block, half).wait()
        columns = pl.ds(half * size, size)
        part = lax.dot_general(
            m_stack[:, columns], x_stack[:, columns], (((1,), (1,)), ((), ())),
            preferred_element_type=jnp.float32,
        )
        similarity = part if similarity is None else similarity + part
    x_best, x_sum = [None] * x_count, [None] * x_count
    m_best, m_sum = [None] * m_count, [None] * m_count

    def join(bests, totals, where, best, score):
        bests[where] = best if bests[where] is None else jnp.maximum(bests[where], best)
        totals[where] = score if totals[where] is None else totals[where] + score

    for m in range(m_count):
        for x in plan[m]:
            block = similarity[m * tokens : (m + 1) * tokens, x * tokens : (x + 1) * tokens]
            x_row, m_row, score = pair_stats(block, slots_ref[at + x], slots_ref[at + x_count + m])
            join(x_best, x_sum, x, x_row, score)
            join(m_best, m_sum, m, m_row, score)
    assemble(x_best, x_sum, m_best, m_sum, *tables, *outs)


def score(name, plan, slots, at, x_blocks, m_blocks, assemble, tables, out_rows):
    arrays = list(x_blocks) + list(m_blocks)
    tokens, width = arrays[0].shape
    vmem = pl.BlockSpec(memory_space=pltpu.VMEM)
    halves = 2
    return pl.pallas_call(
        functools.partial(score_kernel, plan, at, len(x_blocks), len(m_blocks), len(out_rows), assemble),
        in_specs=[pl.BlockSpec(memory_space=pltpu.SMEM)]
        + [pl.BlockSpec(memory_space=pl.ANY)] * len(arrays)
        + [vmem] * len(tables),
        out_specs=[vmem for rows in out_rows],
        out_shape=[jax.ShapeDtypeStruct((rows, tokens), jnp.float32) for rows in out_rows],
        scratch_shapes=[
            pltpu.VMEM((len(x_blocks) * tokens, width), jnp.bfloat16),
            pltpu.VMEM((len(m_blocks) * tokens, width), jnp.bfloat16),
            pltpu.SemaphoreType.DMA((len(arrays), halves)),
        ],
        cost_estimate=pl.CostEstimate(
            flops=2 * len(x_blocks) * len(m_blocks) * tokens * tokens * width,
            bytes_accessed=2 * len(arrays) * tokens * width,
            transcendentals=0,
        ),
        compiler_params=pltpu.CompilerParams(vmem_limit_bytes=VMEM_LIMIT),
        name=name,
    )(slots, *arrays, *tables)


def put(out_ref, *rows):
    out_ref[...] = jnp.concatenate(list(rows) + [jnp.zeros_like(rows[0])] * (8 - len(rows)), axis=0)


def write_near(x_best, x_sum, m_best, m_sum, own_ref, forth_ref, back_ref):
    put(own_ref, x_best[0], x_sum[0], x_best[1], x_sum[1], m_best[0], m_sum[0])
    put(back_ref, m_best[1], m_sum[1])
    put(forth_ref, m_best[2], m_sum[2])


def write_far(x_best, x_sum, m_best, m_sum, near, forth, back, out_ref):
    rows = [
        jnp.maximum(near[0:1], x_best[0]),
        near[1:2] + x_sum[0],
        jnp.maximum(near[4:5], jnp.maximum(forth[0:1], back[0:1])),
        near[5:6] + forth[1:2] + back[1:2],
        jnp.maximum(near[2:3], x_best[1]),
        near[3:4] + x_sum[1],
        x_best[2],
        x_sum[2],
        x_best[3],
        x_sum[3],
        m_best[0],
        m_sum[0],
        m_best[1],
        m_sum[1],
    ]
    out_ref[...] = jnp.concatenate(rows + [jnp.zeros_like(rows[0])] * 2, axis=0)


def sort_kernel(flags_ref, gathered_ref, home_ref, onward_ref, backward_ref):
    mid = flags_ref[0]
    worker = [flags_ref[1], flags_ref[2]]
    facing = [flags_ref[3], flags_ref[4]]

    def row(which, at):
        return gathered_ref[which, pl.ds(at, 1), :]

    def emit(ref, best0, best1, sum0, sum1):
        zero = jnp.zeros_like(best0)
        ref[...] = jnp.concatenate([best0, best1, sum0, sum1, zero, zero, zero, zero], axis=0)

    @pl.when(mid == 1)
    def _():
        emit(home_ref, row(worker[0], 2), row(worker[1], 2), row(worker[0], 3), row(worker[1], 3))
        emit(onward_ref, row(worker[0], 12), row(worker[1], 10), row(worker[0], 13), row(worker[1], 11))
        emit(backward_ref, row(worker[0], 10), row(worker[1], 12), row(worker[0], 11), row(worker[1], 13))

    @pl.when(mid == 0)
    def _():
        best = [jnp.maximum(row(worker[p], 0), row(facing[p], 4)) for p in range(2)]
        total = [row(worker[p], 1) + row(facing[p], 5) for p in range(2)]
        next_best = [jnp.maximum(row(worker[p], 6), row(facing[p], 8)) for p in range(2)]
        next_total = [row(worker[p], 7) + row(facing[p], 9) for p in range(2)]
        nothing = jnp.full_like(best[0], sentinel)
        none = jnp.zeros_like(best[0])
        emit(home_ref, best[0], best[1], total[0], total[1])
        emit(onward_ref, nothing, next_best[1], none, next_total[1])
        emit(backward_ref, next_best[0], nothing, next_total[0], none)


def sort(flags, gathered):
    tokens = gathered.shape[-1]
    vmem = pl.BlockSpec(memory_space=pltpu.VMEM)
    return pl.pallas_call(
        sort_kernel,
        in_specs=[pl.BlockSpec(memory_space=pltpu.SMEM), vmem],
        out_specs=[vmem] * 3,
        out_shape=[jax.ShapeDtypeStruct((8, tokens), jnp.float32)] * 3,
        name="sort_tables",
    )(flags, gathered)


def body(states, lengths):
    tokens = states.shape[2]
    candidates = lengths.shape[1]
    members = lax.axis_size("dev")
    group = lax.axis_index("grp")
    member = lax.axis_index("dev")
    mid = (group % 2) ^ (group // 2 % 2)
    prompt = 1 - mid
    direction = 2 * (group % 2) - 1

    def wanted(which, place):
        return prompt * candidates + which * members + (member + direction * place) % members

    m_group, c_group = group ^ (1 - mid), group ^ mid
    y_group = c_group ^ 3
    slots = [wanted(c_group, 0), wanted(y_group, 0), wanted(m_group, 0), wanted(m_group, -1), wanted(m_group, 1)]
    slots += [wanted(c_group, -1), wanted(y_group, 1), wanted(m_group, -2), wanted(m_group, 2)]
    order = [0, 1, 2, 3, 4, 0, 1, 5, 6, 7, 8]
    flat = lengths.reshape(1, -1)
    chosen = jnp.stack([slots[k] for k in order])[:, None] == lax.broadcasted_iota(jnp.int32, (1, flat.shape[1]), 1)
    slots = jnp.sum(jnp.where(chosen, flat, 0), axis=1)
    first, second = m_group % 4, (m_group ^ 1) % 4
    flags = jnp.stack([mid, first, second, first ^ 3, second ^ 3]).astype(jnp.int32)

    raw = states[:, 0]
    mid_flag = jnp.reshape(mid, (1,)).astype(jnp.int32)
    given = move(pick(mid_flag, raw), 0, 1)
    m_own, c_own = normalize(mid_flag, raw, given)

    c_next = move(c_own, 1)
    y_own = move(c_own, 0, 3)
    m_behind1 = move(m_own, 1)
    m_ahead1 = move(m_own, -1)
    payload, y_own = after(c_next, y_own)
    y_next = move(payload, 0, 3)
    m_behind2 = move(m_behind1, 1)
    m_ahead2 = move(m_ahead1, -1)

    near, forth, back = score(
        "near", [[0, 1]] * 3, slots, 0, [c_own, y_own], [m_own, m_behind1, m_ahead1], write_near, [], [8, 8, 8]
    )
    forth, back, m_ahead2 = after(forth, back, m_ahead2)
    forth = move(forth, 1)
    back = move(back, -1)
    (found,) = score(
        "far", [[0, 1, 3], [0, 1, 2]], slots, 5, [c_own, y_own, c_next, y_next], [m_behind2, m_ahead2],
        write_far, [near, forth, back], [16],
    )
    home, onward, backward = sort(flags, gather(found, 4))
    onward, backward = send_home(onward, 1), send_home(backward, -1)

    here = group * members + member
    columns = lax.broadcasted_iota(jnp.int32, lengths.shape, 1)
    own_lengths = jnp.sum(jnp.where(columns == here, lengths, 0), axis=1)
    best = jnp.maximum(home[:2], jnp.maximum(onward[:2], backward[:2]))
    total = home[2:4] + onward[2:4] + backward[2:4]
    token_valid = lax.broadcasted_iota(jnp.int32, (1, tokens), 1) < own_lengths[:, None]
    return (total[:, :1], jnp.where(token_valid, best, 0.0)[:, None, :])


def solution(mesh):
    in_specs = (P(None, ("grp", "dev"), None, None), P())
    out_specs = (P(None, ("grp", "dev")), P(None, ("grp", "dev"), None))
    return jax.shard_map(body, mesh=mesh, in_specs=in_specs, out_specs=out_specs, check_vma=False)
```

```python
import functools

import jax
import jax.numpy as jnp
from jax import lax
from jax.experimental import pallas as pl
from jax.experimental.pallas import tpu as pltpu
from jax.sharding import PartitionSpec as P


epsilon = 1e-06
sentinel = -4.0
VMEM_LIMIT = 24 * 1024 * 1024


def is_mid(g):
    return (g % 2) ^ (g // 2 % 2) == 1


def sign(g):
    return 2 * (g % 2) - 1


def move(value, mid, outer):
    groups, members = lax.axis_size("grp"), lax.axis_size("dev")
    pairs = []
    for g in range(groups):
        route = mid if is_mid(g) else outer
        if route is not None:
            by, mask = route
            for i in range(members):
                pairs.append((g * members + i, (g ^ mask) * members + (i + sign(g) * by) % members))
    return lax.ppermute(value, ("grp", "dev"), pairs)


def send_home(value, way):
    return move(value, (2 * way, 0), (-way, 0))


def gather(value, size):
    groups = lax.axis_size("grp")
    return lax.all_gather(
        value, "grp", axis_index_groups=[list(range(g, g + size)) for g in range(0, groups, size)]
    )


def after(value, *done):
    return lax.optimization_barrier((value, *done))


def normalize_kernel(flags_ref, states_ref, own_ref, given_ref, loaded, unit, load_sems, sems):
    steps = load_sems.shape[0]
    size = loaded.shape[1] // steps
    mid = flags_ref[0]

    def load(step):
        rows = pl.ds(step * size, size)
        return pltpu.make_async_copy(states_ref.at[:, rows], loaded.at[:, rows], load_sems.at[step])

    def stores(step):
        rows = pl.ds(step * size, size)
        return (
            pltpu.make_async_copy(unit.at[1 - mid, rows], own_ref.at[rows], sems.at[step, 0]),
            pltpu.make_async_copy(unit.at[mid, rows], given_ref.at[rows], sems.at[step, 1]),
        )

    for step in range(steps):
        load(step).start()
    for step in range(steps):
        load(step).wait()
        rows = pl.ds(step * size, size)
        for prompt in range(2):
            values = loaded[prompt, rows].astype(jnp.float32)
            total = jnp.sum(values * values, axis=-1, keepdims=True)
            unit[prompt, rows] = (values * lax.rsqrt(total + epsilon)).astype(jnp.bfloat16)
        for copy in stores(step):
            copy.start()
    for step in range(steps):
        for copy in stores(step):
            copy.wait()


def normalize(flags, states):
    _, tokens, width = states.shape
    steps = 4
    one = jax.ShapeDtypeStruct((tokens, width), jnp.bfloat16)
    hbm = pl.BlockSpec(memory_space=pltpu.HBM)
    return pl.pallas_call(
        normalize_kernel,
        in_specs=[pl.BlockSpec(memory_space=pltpu.SMEM), hbm],
        out_specs=[hbm] * 2,
        out_shape=[one, one],
        scratch_shapes=[
            pltpu.VMEM(states.shape, jnp.bfloat16),
            pltpu.VMEM(states.shape, jnp.bfloat16),
            pltpu.SemaphoreType.DMA((steps,)),
            pltpu.SemaphoreType.DMA((steps, 2)),
        ],
        compiler_params=pltpu.CompilerParams(vmem_limit_bytes=VMEM_LIMIT),
        name="normalize",
    )(flags, states)


def pair_stats(similarity, x_len, m_len):
    down = lax.broadcasted_iota(jnp.int32, similarity.shape, 0)
    lane = lax.broadcasted_iota(jnp.int32, (1, similarity.shape[1]), 1)
    x_best = jnp.max(jnp.where(down < m_len, similarity, sentinel), axis=0, keepdims=True)
    m_best = jnp.max(jnp.where(down < x_len, similarity.T, sentinel), axis=0, keepdims=True)
    x_sum = jnp.sum(jnp.where(lane < x_len, x_best, 0.0), axis=1, keepdims=True)
    m_sum = jnp.sum(jnp.where(lane < m_len, m_best, 0.0), axis=1, keepdims=True)
    x_count = jnp.full((1, 1), x_len, jnp.int32).astype(jnp.float32)
    m_count = jnp.full((1, 1), m_len, jnp.int32).astype(jnp.float32)
    score = 0.5 * (x_sum / x_count + m_sum / m_count)
    return x_best, m_best, jnp.broadcast_to(score, x_best.shape)


def score_kernel(plan, at, choice, x_count, m_count, array_count, out_count, assemble, flags_ref, slots_ref, *refs):
    sources = refs[:array_count]
    tables = refs[array_count : -3 - out_count]
    outs = refs[-3 - out_count : -3]
    x_stack, m_stack, sems = refs[-3:]
    tokens, width = sources[0].shape
    halves = sems.shape[1]
    size = width // halves

    def load(block, half, role):
        stack, row = (x_stack, block) if block < x_count else (m_stack, block - x_count)
        columns = pl.ds(half * size, size)
        return pltpu.make_async_copy(
            sources[choice[block][role]].at[:, columns],
            stack.at[pl.ds(row * tokens, tokens), columns],
            sems.at[block, half],
        )

    for role in range(2):

        @pl.when(flags_ref[0] == 1 - role)
        def _():
            for half in range(halves):
                for block in range(x_count + m_count):
                    load(block, half, role).start()

    similarity = None
    for half in range(halves):
        for block in range(x_count + m_count):
            load(block, half, 0).wait()
        columns = pl.ds(half * size, size)
        part = lax.dot_general(
            m_stack[:, columns], x_stack[:, columns], (((1,), (1,)), ((), ())),
            preferred_element_type=jnp.float32,
        )
        similarity = part if similarity is None else similarity + part
    x_best, x_sum = [None] * x_count, [None] * x_count
    m_best, m_sum = [None] * m_count, [None] * m_count

    def join(bests, totals, where, best, score):
        bests[where] = best if bests[where] is None else jnp.maximum(bests[where], best)
        totals[where] = score if totals[where] is None else totals[where] + score

    for m in range(m_count):
        for x in plan[m]:
            block = similarity[m * tokens : (m + 1) * tokens, x * tokens : (x + 1) * tokens]
            x_row, m_row, score = pair_stats(block, slots_ref[at + x], slots_ref[at + x_count + m])
            join(x_best, x_sum, x, x_row, score)
            join(m_best, m_sum, m, m_row, score)
    assemble(x_best, x_sum, m_best, m_sum, *tables, *outs)


def score(name, plan, flags, slots, at, arrays, x_choice, m_choice, assemble, tables, out_rows):
    tokens, width = arrays[0].shape
    x_count, m_count = len(x_choice), len(m_choice)
    vmem = pl.BlockSpec(memory_space=pltpu.VMEM)
    smem = pl.BlockSpec(memory_space=pltpu.SMEM)
    halves = 2
    kernel = functools.partial(
        score_kernel, plan, at, x_choice + m_choice, x_count, m_count, len(arrays), len(out_rows), assemble
    )
    return pl.pallas_call(
        kernel,
        in_specs=[smem] * 2 + [pl.BlockSpec(memory_space=pltpu.HBM)] * len(arrays) + [vmem] * len(tables),
        out_specs=[vmem for rows in out_rows],
        out_shape=[jax.ShapeDtypeStruct((rows, tokens), jnp.float32) for rows in out_rows],
        scratch_shapes=[
            pltpu.VMEM((x_count * tokens, width), jnp.bfloat16),
            pltpu.VMEM((m_count * tokens, width), jnp.bfloat16),
            pltpu.SemaphoreType.DMA((x_count + m_count, halves)),
        ],
        cost_estimate=pl.CostEstimate(
            flops=2 * x_count * m_count * tokens * tokens * width,
            bytes_accessed=2 * (x_count + m_count) * tokens * width,
            transcendentals=0,
        ),
        compiler_params=pltpu.CompilerParams(vmem_limit_bytes=VMEM_LIMIT),
        name=name,
    )(flags, slots, *arrays, *tables)


def put(out_ref, *rows):
    out_ref[...] = jnp.concatenate(list(rows) + [jnp.zeros_like(rows[0])] * (8 - len(rows)), axis=0)


def write_near(x_best, x_sum, m_best, m_sum, own_ref, forth_ref, back_ref):
    put(own_ref, x_best[0], x_sum[0], x_best[1], x_sum[1], m_best[0], m_sum[0])
    put(back_ref, m_best[1], m_sum[1])
    put(forth_ref, m_best[2], m_sum[2])


def write_far(x_best, x_sum, m_best, m_sum, near, forth, back, out_ref):
    rows = [
        jnp.maximum(near[0:1], x_best[0]),
        near[1:2] + x_sum[0],
        jnp.maximum(near[4:5], jnp.maximum(forth[0:1], back[0:1])),
        near[5:6] + forth[1:2] + back[1:2],
        jnp.maximum(near[2:3], x_best[1]),
        near[3:4] + x_sum[1],
        x_best[2],
        x_sum[2],
        x_best[3],
        x_sum[3],
        m_best[0],
        m_sum[0],
        m_best[1],
        m_sum[1],
    ]
    out_ref[...] = jnp.concatenate(rows + [jnp.zeros_like(rows[0])] * 2, axis=0)


def finish_kernel(slots_ref, here_ref, onward_ref, backward_ref, total_ref, best_ref):
    mid = slots_ref[13]
    worker = [slots_ref[14], slots_ref[15]]
    facing = [slots_ref[16], slots_ref[17]]
    lane = lax.broadcasted_iota(jnp.int32, (1, here_ref.shape[2]), 1)

    def join(parts):
        totals = []
        for prompt in range(2):
            best = [ref[which, pl.ds(at, 1), :] for ref, which, at in parts[prompt]]
            total = [ref[which, pl.ds(at + 1, 1), :] for ref, which, at in parts[prompt]]
            best = functools.reduce(jnp.maximum, best)
            best_ref[prompt] = jnp.where(lane < slots_ref[11 + prompt], best, 0.0)
            totals.append(sum(total[1:], total[0]))
        total_ref[...] = jnp.where(lane == 0, totals[0], totals[1])[:, :2]

    @pl.when(mid == 1)
    def _():
        join(
            [
                [(here_ref, worker[0], 2), (onward_ref, worker[0], 12), (backward_ref, worker[0], 10)],
                [(here_ref, worker[1], 2), (onward_ref, worker[1], 10), (backward_ref, worker[1], 12)],
            ]
        )

    @pl.when(mid == 0)
    def _():
        join(
            [
                [(ref, which, at) for ref, next_at in ((here_ref, 0), (neighbour, 6)) for which, at in
                 ((worker[prompt], next_at), (facing[prompt], next_at + (4 if next_at == 0 else 2)))]
                for prompt, neighbour in ((0, backward_ref), (1, onward_ref))
            ]
        )


def finish(slots, here, onward, backward):
    tokens = here.shape[-1]
    vmem = pl.BlockSpec(memory_space=pltpu.VMEM)
    smem = pl.BlockSpec(memory_space=pltpu.SMEM)
    return pl.pallas_call(
        finish_kernel,
        in_specs=[smem] + [vmem] * 3,
        out_specs=[vmem] * 2,
        out_shape=[jax.ShapeDtypeStruct((1, 2), jnp.float32), jax.ShapeDtypeStruct((2, 1, tokens), jnp.float32)],
        name="finish",
    )(slots, here, onward, backward)


def body(states, lengths):
    tokens = states.shape[2]
    candidates = lengths.shape[1]
    members = lax.axis_size("dev")
    group = lax.axis_index("grp")
    member = lax.axis_index("dev")
    mid = (group % 2) ^ (group // 2 % 2)
    prompt = 1 - mid
    direction = 2 * (group % 2) - 1

    def wanted(which, place):
        return prompt * candidates + which * members + (member + direction * place) % members

    m_group, c_group = group ^ (1 - mid), group ^ mid
    y_group = c_group ^ 3
    slots = [wanted(c_group, 0), wanted(y_group, 0), wanted(m_group, 0), wanted(m_group, -1), wanted(m_group, 1)]
    slots += [wanted(c_group, -1), wanted(y_group, 1), wanted(m_group, -2), wanted(m_group, 2)]
    order = [0, 1, 2, 3, 4, 0, 1, 5, 6, 7, 8]
    here = group * members + member
    wanted_slots = jnp.stack([slots[k] for k in order] + [here, candidates + here])
    flat = lengths.reshape(1, -1)
    chosen = wanted_slots[:, None] == lax.broadcasted_iota(jnp.int32, (1, flat.shape[1]), 1)
    first, second = m_group % 4, (m_group ^ 1) % 4
    slots = jnp.concatenate(
        [jnp.sum(jnp.where(chosen, flat, 0), axis=1), jnp.stack([mid, first, second, first ^ 3, second ^ 3])]
    )
    mid_flag = jnp.reshape(mid, (1,)).astype(jnp.int32)

    own, given = normalize(mid_flag, states[:, 0])
    other = move(given, (0, 1), (0, 1))
    a1 = move(own, (1, 0), (1, 0))
    b1 = move(own, (-1, 0), (0, 3))
    c1 = move(other, (1, 0), (-1, 0))
    d1 = move(other, (0, 3), (1, 0))
    a2 = move(a1, (1, 0), (0, 3))
    c2 = move(c1, (0, 3), (-1, 0))
    payload, d1 = after(b1, d1)
    b2 = move(payload, (-1, 0), None)
    d2 = move(d1, None, (1, 0))

    near, forth, back = score(
        "near", [[0, 1]] * 3, mid_flag, slots, 0, [own, other, a1, b1, c1, d1],
        [(1, 0), (5, 3)], [(0, 1), (2, 5), (3, 4)], write_near, [], [8, 8, 8],
    )
    forth, back, a2 = after(forth, back, a2)
    forth = move(forth, (1, 0), (1, 0))
    back = move(back, (-1, 0), (-1, 0))
    (found,) = score(
        "far", [[0, 1, 3], [0, 1, 2]], mid_flag, slots, 5, [own, other, a1, b1, c1, d1, a2, b2, c2, d2],
        [(1, 0), (5, 3), (4, 2), (8, 6)], [(6, 9), (7, 8)], write_far, [near, forth, back], [16],
    )
    found = gather(found, 4)
    total, best = finish(slots, found, send_home(found, 1), send_home(found, -1))
    return (total.reshape(2, 1), best)


def solution(mesh):
    in_specs = (P(None, ("grp", "dev"), None, None), P())
    out_specs = (P(None, ("grp", "dev")), P(None, ("grp", "dev"), None))
    return jax.shard_map(body, mesh=mesh, in_specs=in_specs, out_specs=out_specs, check_vma=False)
```

```python
import functools

import jax
import jax.numpy as jnp
from jax import lax
from jax.experimental import pallas as pl
from jax.experimental.pallas import tpu as pltpu
from jax.sharding import PartitionSpec as P


epsilon = 1e-06
sentinel = -4.0
VMEM_LIMIT = 24 * 1024 * 1024


def is_mid(g):
    return (g % 2) ^ (g // 2 % 2) == 1


def sign(g):
    return 2 * (g % 2) - 1


def move(value, mid, outer):
    groups, members = lax.axis_size("grp"), lax.axis_size("dev")
    pairs = []
    for g in range(groups):
        route = mid if is_mid(g) else outer
        if route is not None:
            by, mask = route
            for i in range(members):
                pairs.append((g * members + i, (g ^ mask) * members + (i + sign(g) * by) % members))
    return lax.ppermute(value, ("grp", "dev"), pairs)


def send_home(value, way):
    return move(value, (2 * way, 0), (-way, 0))


def gather(value, size):
    groups = lax.axis_size("grp")
    return lax.all_gather(
        value, "grp", axis_index_groups=[list(range(g, g + size)) for g in range(0, groups, size)]
    )


def after(value, *done):
    return lax.optimization_barrier((value, *done))


def normalize_kernel(flags_ref, states_ref, own_ref, given_ref, loaded, unit, load_sems, sems):
    steps = load_sems.shape[0]
    size = loaded.shape[1] // steps
    mid = flags_ref[0]

    def load(step):
        rows = pl.ds(step * size, size)
        return pltpu.make_async_copy(states_ref.at[:, rows], loaded.at[:, rows], load_sems.at[step])

    def stores(step):
        rows = pl.ds(step * size, size)
        return (
            pltpu.make_async_copy(unit.at[1 - mid, rows], own_ref.at[rows], sems.at[step, 0]),
            pltpu.make_async_copy(unit.at[mid, rows], given_ref.at[rows], sems.at[step, 1]),
        )

    for step in range(steps):
        load(step).start()
    for step in range(steps):
        load(step).wait()
        rows = pl.ds(step * size, size)
        for prompt in range(2):
            values = loaded[prompt, rows].astype(jnp.float32)
            total = jnp.sum(values * values, axis=-1, keepdims=True)
            unit[prompt, rows] = (values * lax.rsqrt(total + epsilon)).astype(jnp.bfloat16)
        for copy in stores(step):
            copy.start()
    for step in range(steps):
        for copy in stores(step):
            copy.wait()


def normalize(flags, states):
    _, tokens, width = states.shape
    steps = 4
    one = jax.ShapeDtypeStruct((tokens, width), jnp.bfloat16)
    hbm = pl.BlockSpec(memory_space=pltpu.HBM)
    return pl.pallas_call(
        normalize_kernel,
        in_specs=[pl.BlockSpec(memory_space=pltpu.SMEM), hbm],
        out_specs=[hbm] * 2,
        out_shape=[one, one],
        scratch_shapes=[
            pltpu.VMEM(states.shape, jnp.bfloat16),
            pltpu.VMEM(states.shape, jnp.bfloat16),
            pltpu.SemaphoreType.DMA((steps,)),
            pltpu.SemaphoreType.DMA((steps, 2)),
        ],
        compiler_params=pltpu.CompilerParams(vmem_limit_bytes=VMEM_LIMIT),
        name="normalize",
    )(flags, states)


def pair_stats(similarity, x_len, m_len):
    down = lax.broadcasted_iota(jnp.int32, similarity.shape, 0)
    lane = lax.broadcasted_iota(jnp.int32, (1, similarity.shape[1]), 1)
    x_best = jnp.max(jnp.where(down < m_len, similarity, sentinel), axis=0, keepdims=True)
    m_best = jnp.max(jnp.where(down < x_len, similarity.T, sentinel), axis=0, keepdims=True)
    x_sum = jnp.sum(jnp.where(lane < x_len, x_best, 0.0), axis=1, keepdims=True)
    m_sum = jnp.sum(jnp.where(lane < m_len, m_best, 0.0), axis=1, keepdims=True)
    x_count = jnp.full((1, 1), x_len, jnp.int32).astype(jnp.float32)
    m_count = jnp.full((1, 1), m_len, jnp.int32).astype(jnp.float32)
    score = 0.5 * (x_sum / x_count + m_sum / m_count)
    return x_best, m_best, jnp.broadcast_to(score, x_best.shape)


def score_kernel(plan, at, choice, x_count, m_count, array_count, out_count, assemble, flags_ref, slots_ref, *refs):
    sources = refs[:array_count]
    tables = refs[array_count : -3 - out_count]
    outs = refs[-3 - out_count : -3]
    x_stack, m_stack, sems = refs[-3:]
    tokens, width = sources[0].shape
    halves = sems.shape[1]
    size = width // halves

    def load(block, half, role):
        stack, row = (x_stack, block) if block < x_count else (m_stack, block - x_count)
        columns = pl.ds(half * size, size)
        return pltpu.make_async_copy(
            sources[choice[block][role]].at[:, columns],
            stack.at[pl.ds(row * tokens, tokens), columns],
            sems.at[block, half],
        )

    for role in range(2):

        @pl.when(flags_ref[0] == 1 - role)
        def _():
            for half in range(halves):
                for block in range(x_count + m_count):
                    load(block, half, role).start()

    similarity = None
    for half in range(halves):
        for block in range(x_count + m_count):
            load(block, half, 0).wait()
        columns = pl.ds(half * size, size)
        part = lax.dot_general(
            m_stack[:, columns], x_stack[:, columns], (((1,), (1,)), ((), ())),
            preferred_element_type=jnp.float32,
        )
        similarity = part if similarity is None else similarity + part
    x_best, x_sum = [None] * x_count, [None] * x_count
    m_best, m_sum = [None] * m_count, [None] * m_count

    def join(bests, totals, where, best, score):
        bests[where] = best if bests[where] is None else jnp.maximum(bests[where], best)
        totals[where] = score if totals[where] is None else totals[where] + score

    for m in range(m_count):
        for x in plan[m]:
            block = similarity[m * tokens : (m + 1) * tokens, x * tokens : (x + 1) * tokens]
            x_row, m_row, score = pair_stats(block, slots_ref[at + x], slots_ref[at + x_count + m])
            join(x_best, x_sum, x, x_row, score)
            join(m_best, m_sum, m, m_row, score)
    assemble(x_best, x_sum, m_best, m_sum, *tables, *outs)


def score(name, plan, flags, slots, at, arrays, x_choice, m_choice, assemble, tables, out_rows, weight=1):
    tokens, width = arrays[0].shape
    x_count, m_count = len(x_choice), len(m_choice)
    vmem = pl.BlockSpec(memory_space=pltpu.VMEM)
    smem = pl.BlockSpec(memory_space=pltpu.SMEM)
    halves = 2
    kernel = functools.partial(
        score_kernel, plan, at, x_choice + m_choice, x_count, m_count, len(arrays), len(out_rows), assemble
    )
    return pl.pallas_call(
        kernel,
        in_specs=[smem] * 2 + [pl.BlockSpec(memory_space=pltpu.HBM)] * len(arrays) + [vmem] * len(tables),
        out_specs=[vmem for rows in out_rows],
        out_shape=[jax.ShapeDtypeStruct((rows, tokens), jnp.float32) for rows in out_rows],
        scratch_shapes=[
            pltpu.VMEM((x_count * tokens, width), jnp.bfloat16),
            pltpu.VMEM((m_count * tokens, width), jnp.bfloat16),
            pltpu.SemaphoreType.DMA((x_count + m_count, halves)),
        ],
        cost_estimate=pl.CostEstimate(
            flops=weight * 2 * x_count * m_count * tokens * tokens * width,
            bytes_accessed=weight * 2 * (x_count + m_count) * tokens * width,
            transcendentals=0,
        ),
        compiler_params=pltpu.CompilerParams(vmem_limit_bytes=VMEM_LIMIT),
        name=name,
    )(flags, slots, *arrays, *tables)


def put(out_ref, *rows):
    out_ref[...] = jnp.concatenate(list(rows) + [jnp.zeros_like(rows[0])] * (8 - len(rows)), axis=0)


def write_near(x_best, x_sum, m_best, m_sum, own_ref, forth_ref, back_ref):
    put(own_ref, x_best[0], x_sum[0], x_best[1], x_sum[1], m_best[0], m_sum[0])
    put(back_ref, m_best[1], m_sum[1])
    put(forth_ref, m_best[2], m_sum[2])


def write_far(x_best, x_sum, m_best, m_sum, near, out_ref):
    rows = [
        jnp.maximum(near[0:1], x_best[0]),
        near[1:2] + x_sum[0],
        near[4:5],
        near[5:6],
        jnp.maximum(near[2:3], x_best[1]),
        near[3:4] + x_sum[1],
        x_best[2],
        x_sum[2],
        x_best[3],
        x_sum[3],
        m_best[0],
        m_sum[0],
        m_best[1],
        m_sum[1],
    ]
    out_ref[...] = jnp.concatenate(rows + [jnp.zeros_like(rows[0])] * 2, axis=0)


def finish_kernel(slots_ref, here_ref, onward_ref, backward_ref, total_ref, best_ref):
    mid = slots_ref[13]
    worker = [slots_ref[14], slots_ref[15]]
    facing = [slots_ref[16], slots_ref[17]]
    lane = lax.broadcasted_iota(jnp.int32, (1, here_ref.shape[2]), 1)

    def join(parts):
        totals = []
        for prompt in range(2):
            best = [ref[which, pl.ds(at, 1), :] for ref, which, at in parts[prompt]]
            total = [ref[which, pl.ds(at + 1, 1), :] for ref, which, at in parts[prompt]]
            best = functools.reduce(jnp.maximum, best)
            best_ref[prompt] = jnp.where(lane < slots_ref[11 + prompt], best, 0.0)
            totals.append(sum(total[1:], total[0]))
        total_ref[...] = jnp.where(lane == 0, totals[0], totals[1])[:, :2]

    @pl.when(mid == 1)
    def _():
        join(
            [
                [(here_ref, worker[0], 2), (onward_ref, worker[0], 12), (backward_ref, worker[0], 10)],
                [(here_ref, worker[1], 2), (onward_ref, worker[1], 10), (backward_ref, worker[1], 12)],
            ]
        )

    @pl.when(mid == 0)
    def _():
        join(
            [
                [(ref, which, at) for ref, next_at in ((here_ref, 0), (neighbour, 6)) for which, at in
                 ((worker[prompt], next_at), (facing[prompt], next_at + (4 if next_at == 0 else 2)))]
                for prompt, neighbour in ((0, backward_ref), (1, onward_ref))
            ]
        )


def finish(slots, here, onward, backward):
    tokens = here.shape[-1]
    vmem = pl.BlockSpec(memory_space=pltpu.VMEM)
    smem = pl.BlockSpec(memory_space=pltpu.SMEM)
    return pl.pallas_call(
        finish_kernel,
        in_specs=[smem] + [vmem] * 3,
        out_specs=[vmem] * 2,
        out_shape=[jax.ShapeDtypeStruct((1, 2), jnp.float32), jax.ShapeDtypeStruct((2, 1, tokens), jnp.float32)],
        name="finish",
    )(slots, here, onward, backward)


def body(states, lengths):
    tokens = states.shape[2]
    candidates = lengths.shape[1]
    members = lax.axis_size("dev")
    group = lax.axis_index("grp")
    member = lax.axis_index("dev")
    mid = (group % 2) ^ (group // 2 % 2)
    prompt = 1 - mid
    direction = 2 * (group % 2) - 1

    def wanted(which, place):
        return prompt * candidates + which * members + (member + direction * place) % members

    m_group, c_group = group ^ (1 - mid), group ^ mid
    y_group = c_group ^ 3
    slots = [wanted(c_group, 0), wanted(y_group, 0), wanted(m_group, 0), wanted(m_group, -1), wanted(m_group, 1)]
    slots += [wanted(c_group, -1), wanted(y_group, 1), wanted(m_group, -2), wanted(m_group, 2)]
    order = [0, 1, 2, 3, 4, 0, 1, 5, 6, 7, 8]
    here = group * members + member
    wanted_slots = jnp.stack([slots[k] for k in order] + [here, candidates + here])
    flat = lengths.reshape(1, -1)
    chosen = wanted_slots[:, None] == lax.broadcasted_iota(jnp.int32, (1, flat.shape[1]), 1)
    first, second = m_group % 4, (m_group ^ 1) % 4
    slots = jnp.concatenate(
        [jnp.sum(jnp.where(chosen, flat, 0), axis=1), jnp.stack([mid, first, second, first ^ 3, second ^ 3])]
    )
    mid_flag = jnp.reshape(mid, (1,)).astype(jnp.int32)

    own, given = normalize(mid_flag, states[:, 0])
    other = move(given, (0, 1), (0, 1))
    a1 = move(own, (1, 0), (1, 0))
    b1 = move(own, (-1, 0), (0, 3))
    c1 = move(other, (1, 0), (-1, 0))
    d1 = move(other, (0, 3), (1, 0))
    a2 = move(a1, (1, 0), (0, 3))
    c2 = move(c1, (0, 3), (-1, 0))
    payload, d1 = after(b1, d1)
    b2 = move(payload, (-1, 0), None)
    d2 = move(d1, None, (1, 0))

    near, forth, back = score(
        "near", [[0, 1]] * 3, mid_flag, slots, 0, [own, other, a1, b1, c1, d1],
        [(1, 0), (5, 3)], [(0, 1), (2, 5), (3, 4)], write_near, [], [8, 8, 8], 10,
    )
    forth, back, a2 = after(forth, back, a2)
    forth = move(forth, (1, 0), (1, 0))
    back = move(back, (-1, 0), (-1, 0))
    (found,) = score(
        "far", [[0, 1, 3], [0, 1, 2]], mid_flag, slots, 5, [own, other, a1, b1, c1, d1, d2, b2, c2, a2],
        [(1, 0), (5, 3), (4, 2), (8, 9)], [(9, 6), (7, 8)], write_far, [near], [16],
    )
    row = lax.broadcasted_iota(jnp.int32, (found.shape[0], 1), 0)
    best = jnp.maximum(found, jnp.maximum(forth[:1], back[:1]))
    total = found + forth[1:2] + back[1:2]
    found = gather(jnp.where(row == 2, best, jnp.where(row == 3, total, found)), 4)
    total, best = finish(slots, found, send_home(found, 1), send_home(found, -1))
    return (total.reshape(2, 1), best)


def solution(mesh):
    in_specs = (P(None, ("grp", "dev"), None, None), P())
    out_specs = (P(None, ("grp", "dev")), P(None, ("grp", "dev"), None))
    return jax.shard_map(body, mesh=mesh, in_specs=in_specs, out_specs=out_specs, check_vma=False)
```
